32 devices in a mesh: grp: 2 (over x), chan: 16 (over z, y, core).
Axes of the slice: x: 2, y: 2, z: 4, core: 2. Of those that a mesh axis runs over, the one named last changes fastest.
Arguments:
- voltages: bfloat16 [2, 2048, 12032], P(None, ('grp', 'chan')), parts along dimension 1, may hold values from -6 to 6
- fir_taps: bfloat16 [16, 256], replicated, may hold values from -1.5 to 1.5
- positions: float32 [2, 512], replicated, may hold values from -40 to 40
- cal_amp: float32 [512, 16], P('grp'), parts along dimension 0, may hold values from 0.5 to 2
- cal_phase: float32 [512, 16], P('grp'), parts along dimension 0, may hold values from -3.140625 to 3.140625
- cal_index: int32 [1024], replicated, may hold values from 0 to 255
- owner_counts: int32 [32], P('grp'), parts along dimension 0, may hold values from 0 to 32, as said below
- tile_owner: int32 [32], P('grp'), parts along dimension 0, may hold values from 0 to 15, each once
Outputs:
- owner_images: float32 [32, 16, 256], P(('grp', 'chan')), parts along dimension 0
- subband_autos: float32 [32, 1024], P(('grp', 'chan')), parts along dimension 0
The draws below stay inside these ranges and needn't reach their ends.
There are 2 independent parts, one for each index of `grp`. The reference program is written for one: setup_inputs(seed, part) draws one part's arguments, and reference() takes and returns one part's arrays. A program takes and returns all parts, laid end to end along the dimension named above; an argument that names none is the same for every part. Nothing has to cross between parts.
Inputs may be any that keep to these rules, and one draw needn't show every extreme that they name: `owner_counts`: the counts sum to 256; one subband holds exactly 32 channels and one holds none. `tile_owner`: A permutation of the tiles.
All inputs are finite; a program needn't handle non-finite values.
Results may differ from the reference program's by a relative error of at most 0.0064.
Values may be sent and summed in bfloat16 or wider, within the bound.
A program may use at most 192 MiB of HBM per device.

```python
import math
import jax
import jax.numpy as jnp
from jax import lax

STA = 512
NIN = 1024
CH = 256
AVG = 16
GROUPS = 16
CH_DEV = 16
SB = 16
BLOCKS = 2
SPEC = 32
TAPS = 16
SAMP = 12032
SIDE = 64
PIX = 4096
TILES = 16
TPIX = 256
NCAL = 256
N_CHAN = 16


def draw_owner_counts(key, part):
    key = jax.random.fold_in(key, 7)
    order_key, change_key = jax.random.split(key)
    shuffled = jax.random.permutation(order_key, N_CHAN)
    paired = N_CHAN // 2
    changes = jax.random.randint(change_key, (paired,), -CH_DEV, CH_DEV + 1)
    changes = changes.at[0].set(CH_DEV)
    counts = jnp.zeros((N_CHAN,), jnp.int32)
    counts = counts.at[shuffled[:paired]].set(CH_DEV + changes)
    counts = counts.at[shuffled[paired:]].set(CH_DEV - changes)
    return counts


def set_ends(entries, rng, low, top_value):
    longest = entries.shape.index(max(entries.shape))
    spots = []
    for shift in (0, 1):
        where = [jax.random.randint(jax.random.fold_in(rng, axis), (), 0, length) for axis, length in enumerate(entries.shape)]
        where[longest] = (where[longest] + shift) % entries.shape[longest]
        spots.append(tuple(where))
    return entries.at[spots[0]].set(low).at[spots[1]].set(top_value)


def level_of(rng, dims, cuts, low, top_value):
    factor_of = 1.0
    for dim, blocks in cuts:
        draws = jax.random.uniform(jax.random.fold_in(jax.random.fold_in(rng, 6), dim), (blocks,), jnp.float32, low / len(cuts), top_value / len(cuts))
        factor_of = factor_of * jnp.repeat(jnp.exp(draws), dims[dim] // blocks).reshape((-1,) + (1,) * (len(dims) - 1 - dim))
    return factor_of


def normal_values(rng, extent, scale, most, cuts=(), kind=jnp.bfloat16):
    entries = jax.random.normal(rng, extent, jnp.float32) * scale
    if len(cuts) > 0:
        entries = level_of(rng, extent, cuts, -0.22, 0.18) * entries
    return jnp.clip(entries, min=-most, max=most).astype(kind)


def setup_inputs(seed: int = 0, part: int = 0) -> dict:
    arg_keys = jax.random.split(jax.random.key(seed), 9)
    own_keys = jax.random.split(jax.random.fold_in(arg_keys[8], part), 9)
    return {
        "voltages": normal_values(own_keys[0], (2, NIN, SAMP), 1.0, 6.0, ((1, 16),)),
        "fir_taps": normal_values(arg_keys[1], (TAPS, CH), TAPS ** -0.5, 1.5),
        "positions": jnp.clip(jax.random.uniform(arg_keys[2], (2, STA), jnp.float32, -40.0, 40.0), -40.0, 40.0),
        "cal_amp": jnp.clip(jnp.exp(jax.random.uniform(own_keys[3], (NCAL, GROUPS), jnp.float32, math.log(0.5), math.log(2.0))), 0.5, 2.0),
        "cal_phase": jnp.clip(jax.random.uniform(own_keys[4], (NCAL, GROUPS), jnp.float32, -3.140625, 3.140625), -3.140625, 3.140625),
        "cal_index": set_ends(jax.random.randint(arg_keys[5], (NIN,), 0, NCAL), jax.random.fold_in(arg_keys[5], 1), 0, NCAL - 1).astype(jnp.int32),
        "owner_counts": draw_owner_counts(jax.random.fold_in(jax.random.fold_in(arg_keys[8], part), 71), part),
        "tile_owner": jax.random.permutation(own_keys[7], TILES).astype(jnp.int32),
    }


highest = lax.Precision.HIGHEST

def dft_table(length):
    indices = jnp.arange(length, dtype=jnp.int32)
    products = indices[:, None] * indices[None, :] % length
    angles = products.astype(jnp.float32) * jnp.float32(2.0 * math.pi / length)
    scaling = jnp.float32(1.0 / math.sqrt(length))
    cosine = jnp.cos(angles) * scaling
    sine_part = jnp.sin(angles) * scaling
    upper_half = jnp.stack([cosine, sine_part], axis=1)
    lower_half = jnp.stack([-sine_part, cosine], axis=1)
    return jnp.stack([upper_half, lower_half], axis=1).astype(jnp.bfloat16)

def steering_table(positions, side):
    pixel_ids = jnp.arange(side * side, dtype=jnp.int32)
    centre = side // 2
    across = (pixel_ids // side - centre).astype(jnp.float32) / jnp.float32(side)
    upward = (pixel_ids % side - centre).astype(jnp.float32) / jnp.float32(side)
    east_pos = jnp.repeat(positions[0], 2)
    north_pos = jnp.repeat(positions[1], 2)
    phases = jnp.float32(2.0 * math.pi) * (east_pos[:, None] * across[None, :] + north_pos[:, None] * upward[None, :])
    return jnp.stack([jnp.cos(phases), -jnp.sin(phases)])

def filter_block(voltage, fir_taps, first_spectrum, spectra_count):
    taps_total = fir_taps.shape[0]
    length = fir_taps.shape[1]
    span_len = (spectra_count + taps_total - 1) * length
    window = voltage[:, :, first_spectrum * length:first_spectrum * length + span_len]
    window = window.reshape(voltage.shape[0], voltage.shape[1], spectra_count + taps_total - 1, length)
    summed = jnp.zeros((voltage.shape[0], voltage.shape[1], spectra_count, length), jnp.float32)
    for tap_index in range(taps_total):
        summed = summed + window[:, :, tap_index:tap_index + spectra_count, :].astype(jnp.float32) * fir_taps[tap_index].astype(jnp.float32)
    return summed.astype(jnp.bfloat16)

def reference(voltages, fir_taps, positions, cal_amp, cal_phase, cal_index, owner_counts, tile_owner):
    dft_rows = dft_table(CH).astype(jnp.float32)
    pieces = []
    for block_index in range(BLOCKS):
        filtered = filter_block(voltages, fir_taps, block_index * SB, SB)
        flattened = filtered.astype(jnp.float32).reshape(2, NIN * SB, CH)
        spectra = jnp.einsum('qrk,cpqk->cpr', flattened, dft_rows, precision=highest).astype(jnp.bfloat16)
        pieces.append(spectra.reshape(CH, 2, NIN, SB))
    channel_data = jnp.concatenate(pieces, axis=3).astype(jnp.float32)
    chan_power = lax.optimization_barrier(jnp.sum(channel_data * channel_data, axis=(1, 3))) / jnp.float32(SPEC)
    offsets = (jnp.cumsum(owner_counts) - owner_counts).astype(jnp.int32)
    chan_ids = jnp.arange(CH, dtype=jnp.int32)
    member = ((chan_ids[None, :] >= offsets[:, None]) & (chan_ids[None, :] < (offsets + owner_counts)[:, None])).astype(jnp.float32)
    divisor = jnp.maximum(owner_counts, 1).astype(jnp.float32)
    subband_autos = jnp.dot(member, chan_power, precision=highest) / divisor[:, None]
    cal_ids = jnp.arange(NCAL, dtype=jnp.int32)
    selection = (cal_index[:, None] == cal_ids[None, :]).astype(jnp.float32)
    real_gain = jnp.dot(selection, cal_amp * jnp.cos(cal_phase), precision=highest).T
    imag_gain = jnp.dot(selection, cal_amp * jnp.sin(cal_phase), precision=highest).T
    steering = steering_table(positions, SIDE)
    steer_flat = steering.reshape(2 * NIN, PIX)
    image_scale = jnp.float32(math.sqrt(SPEC * AVG) / NIN)
    spectra_inverse = jnp.float32(1.0 / (SPEC * AVG))
    input_ids = jnp.arange(NIN, dtype=jnp.int32)
    on_diagonal = input_ids[:, None] == input_ids[None, :]

    def one_group(group_index):
        members = lax.dynamic_slice_in_dim(channel_data, group_index * AVG, AVG, 0)
        real_part = jnp.transpose(members[:, 0], (1, 0, 2)).reshape(NIN, AVG * SPEC)
        imag_part = jnp.transpose(members[:, 1], (1, 0, 2)).reshape(NIN, AVG * SPEC)
        joined = jnp.concatenate([real_part, imag_part], axis=1)
        turned = jnp.concatenate([imag_part, -real_part], axis=1)
        vis_real = jnp.dot(joined, joined.T, precision=highest) * spectra_inverse
        vis_imag = jnp.dot(turned, joined.T, precision=highest) * spectra_inverse
        gain_re = real_gain[group_index]
        gain_im = imag_gain[group_index]
        pair_real = gain_re[:, None] * gain_re[None, :] + gain_im[:, None] * gain_im[None, :]
        pair_imag = gain_im[:, None] * gain_re[None, :] - gain_re[:, None] * gain_im[None, :]
        cal_real = jnp.where(on_diagonal, jnp.float32(0.0), pair_real * vis_real - pair_imag * vis_imag)
        cal_imag = jnp.where(on_diagonal, jnp.float32(0.0), pair_real * vis_imag + pair_imag * vis_real)
        upper_rows = jnp.concatenate([cal_real, -cal_imag], axis=1)
        lower_rows = jnp.concatenate([cal_imag, cal_real], axis=1)
        left_rows = jnp.concatenate([upper_rows, lower_rows], axis=0)
        beam_sums = jnp.dot(left_rows, steer_flat, precision=highest)
        return image_scale * lax.optimization_barrier(jnp.sum(steering[0] * beam_sums[:NIN] + steering[1] * beam_sums[NIN:], axis=0))
    images = lax.map(one_group, jnp.arange(GROUPS, dtype=jnp.int32))
    tile_ids = jnp.arange(TILES, dtype=jnp.int32)
    chooser = (tile_owner[None, :] == tile_ids[:, None]).astype(jnp.float32)
    owner_images = jnp.einsum('dt,gtx->dgx', chooser, images.reshape(GROUPS, TILES, TPIX), precision=highest)
    return (owner_images, subband_autos)
```

```python
import math

import jax
import jax.numpy as jnp
from jax import lax
from jax.sharding import PartitionSpec as P

CH = 256
AVG = 16
GROUPS = 16
SPEC = 32
TAPS = 16
SIDE = 64
PIX = 4096
NCAL = 256

highest = lax.Precision.HIGHEST


def dft_table(length):
    indices = jnp.arange(length, dtype=jnp.int32)
    products = indices[:, None] * indices[None, :] % length
    angles = products.astype(jnp.float32) * jnp.float32(2.0 * math.pi / length)
    scaling = jnp.float32(1.0 / math.sqrt(length))
    cosine = jnp.cos(angles) * scaling
    sine_part = jnp.sin(angles) * scaling
    upper_half = jnp.stack([cosine, sine_part], axis=1)
    lower_half = jnp.stack([-sine_part, cosine], axis=1)
    return jnp.stack([upper_half, lower_half], axis=1).astype(jnp.bfloat16)


def steering_tables(positions):
    steps = (jnp.arange(SIDE, dtype=jnp.float32) - SIDE // 2) / jnp.float32(SIDE)
    turn = jnp.float32(2.0 * math.pi)
    east = turn * (steps[:, None] * positions[0][None, :])
    north = turn * (steps[:, None] * positions[1][None, :])
    east_cos, east_sin = lax.optimization_barrier((jnp.cos(east), jnp.sin(east)))
    north_cos, north_sin = lax.optimization_barrier((jnp.cos(north), jnp.sin(north)))
    cosine = east_cos[:, None] * north_cos[None] - east_sin[:, None] * north_sin[None]
    sine = east_sin[:, None] * north_cos[None] + east_cos[:, None] * north_sin[None]
    stations = positions.shape[1]
    return (
        cosine.reshape(PIX, stations).astype(jnp.bfloat16),
        sine.reshape(PIX, stations).astype(jnp.bfloat16),
    )


def polyphase(voltage, fir_taps):
    length = fir_taps.shape[1]
    window = voltage.reshape(voltage.shape[0], voltage.shape[1], -1, length)
    summed = jnp.zeros((voltage.shape[0], voltage.shape[1], SPEC, length), jnp.float32)
    for tap_index in range(TAPS):
        summed = summed + window[:, :, tap_index : tap_index + SPEC, :].astype(
            jnp.float32
        ) * fir_taps[tap_index].astype(jnp.float32)
    return summed.astype(jnp.bfloat16)


def local(voltages, fir_taps, positions, cal_amp, cal_phase, cal_index, owner_counts, tile_owner):
    devices = lax.axis_size("chan")
    myself = lax.axis_index("chan")
    in_dev = voltages.shape[1]
    st_dev = in_dev // 2
    stations = st_dev * devices
    chan_dev = CH // devices
    per_group = AVG // chan_dev

    my_index = lax.dynamic_slice_in_dim(cal_index, myself * in_dev, in_dev, 0)
    selection = (my_index[:, None] == jnp.arange(NCAL, dtype=jnp.int32)[None, :]).astype(jnp.float32)
    gain_re = jnp.dot(selection, cal_amp * jnp.cos(cal_phase), precision=highest).T
    gain_im = jnp.dot(selection, cal_amp * jnp.sin(cal_phase), precision=highest).T

    filtered = polyphase(voltages, fir_taps)
    spectra = jnp.einsum(
        "qrk,cpqk->cpr",
        filtered.reshape(2, in_dev * SPEC, CH),
        dft_table(CH),
        preferred_element_type=jnp.float32,
    ).astype(jnp.bfloat16)
    values = spectra.astype(jnp.float32).reshape(GROUPS, AVG, 2, st_dev, 2, SPEC)

    powers = jnp.sum(values * values, axis=(2, 5))
    power_rows = powers.reshape(CH, in_dev) / jnp.float32(SPEC)
    offsets = jnp.cumsum(owner_counts) - owner_counts
    chan_ids = jnp.arange(CH, dtype=jnp.int32)
    member = (
        (chan_ids[None, :] >= offsets[:, None])
        & (chan_ids[None, :] < (offsets + owner_counts)[:, None])
    ).astype(jnp.float32)
    divisor = jnp.maximum(owner_counts, 1).astype(jnp.float32)
    sub_rows = jnp.dot(member, power_rows, precision=highest) / divisor[:, None]

    gre = gain_re.reshape(GROUPS, 1, st_dev, 2, 1)
    gim = gain_im.reshape(GROUPS, 1, st_dev, 2, 1)
    cal_re = values[:, :, 0] * gre - values[:, :, 1] * gim
    cal_im = values[:, :, 0] * gim + values[:, :, 1] * gre
    sum_re = cal_re[:, :, :, 0] + cal_re[:, :, :, 1]
    sum_im = cal_im[:, :, :, 0] + cal_im[:, :, :, 1]
    crossed = 2.0 * (
        cal_re[:, :, :, 0] * cal_re[:, :, :, 1] + cal_im[:, :, :, 0] * cal_im[:, :, :, 1]
    )
    cross_power = jnp.sum(crossed, axis=(1, 2, 3))
    outgoing = jnp.stack([sum_re, sum_im], axis=0).astype(jnp.bfloat16)
    outgoing = outgoing.reshape(2, devices, chan_dev, st_dev, SPEC)
    outgoing = jnp.transpose(outgoing, (1, 0, 3, 2, 4)).reshape(
        devices, 2, st_dev, chan_dev * SPEC
    )
    incoming = lax.all_to_all(outgoing, "chan", split_axis=0, concat_axis=0, tiled=True)

    cosine, sine = steering_tables(positions)
    joined = jnp.transpose(incoming, (1, 0, 2, 3)).reshape(2, stations, chan_dev * SPEC)
    real, imag = joined[0], joined[1]
    contract = (((1,), (1,)), ((), ()))
    along = jnp.concatenate([real, imag], axis=1)
    turned = jnp.concatenate([imag, -real], axis=1)
    even = lax.dot_general(along, along, contract, preferred_element_type=jnp.float32)
    odd = lax.dot_general(turned, along, contract, preferred_element_type=jnp.float32)
    station_ids = jnp.arange(stations, dtype=jnp.int32)
    on_diagonal = station_ids[:, None] == station_ids[None, :]
    even = jnp.where(on_diagonal, jnp.float32(0.0), even).astype(jnp.bfloat16)
    odd = jnp.where(on_diagonal, jnp.float32(0.0), -2.0 * odd).astype(jnp.bfloat16)
    first = jnp.dot(cosine, even, preferred_element_type=jnp.float32) + jnp.dot(
        sine, odd, preferred_element_type=jnp.float32
    )
    second = jnp.dot(sine, even, preferred_element_type=jnp.float32)
    image = jnp.sum(
        cosine.astype(jnp.float32) * first + sine.astype(jnp.float32) * second, axis=1
    )

    tile_pix = PIX // devices
    device_ids = jnp.arange(devices, dtype=jnp.int32)
    tile_of = jnp.sum(
        jnp.where(tile_owner[None, :] == device_ids[:, None], device_ids[None, :], 0), axis=1
    )
    tiles = image.reshape(devices, tile_pix)[tile_of]
    last = jnp.concatenate(
        [tiles, sub_rows, jnp.broadcast_to(cross_power[None], (devices, GROUPS))], axis=1
    )
    arrived = lax.all_to_all(last, "chan", split_axis=0, concat_axis=0, tiled=True)
    scale = jnp.float32(1.0 / (SPEC * AVG) * math.sqrt(SPEC * AVG) / (2 * stations))
    pieces = jnp.sum(arrived[:, :tile_pix].reshape(GROUPS, per_group, tile_pix), axis=1)
    constant = jnp.sum(arrived[:, tile_pix + in_dev :], axis=0)
    result = scale * (pieces + constant[:, None])
    autos = arrived[:, tile_pix : tile_pix + in_dev].reshape(1, devices * in_dev)
    return (result[None], autos)


def solution(mesh):
    in_specs = (
        P(None, ("grp", "chan"), None),
        P(),
        P(),
        P("grp", None),
        P("grp", None),
        P(),
        P("grp"),
        P("grp"),
    )
    out_specs = (P(("grp", "chan"), None, None), P(("grp", "chan"), None))
    return jax.shard_map(local, mesh=mesh, in_specs=in_specs, out_specs=out_specs, check_vma=False)
```

```python
import math

import jax
import jax.numpy as jnp
from jax import lax
from jax.experimental import pallas as pl
from jax.experimental.pallas import tpu as pltpu
from jax.sharding import PartitionSpec as P

CH = 256
AVG = 16
GROUPS = 16
SPEC = 32
TAPS = 16
SIDE = 64
PIX = 4096
NCAL = 256

highest = lax.Precision.HIGHEST


def dft_table(length):
    indices = jnp.arange(length, dtype=jnp.int32)
    products = indices[:, None] * indices[None, :] % length
    angles = products.astype(jnp.float32) * jnp.float32(2.0 * math.pi / length)
    scaling = jnp.float32(1.0 / math.sqrt(length))
    cosine = jnp.cos(angles) * scaling
    sine_part = jnp.sin(angles) * scaling
    upper_half = jnp.stack([cosine, sine_part], axis=1)
    lower_half = jnp.stack([-sine_part, cosine], axis=1)
    return jnp.stack([upper_half, lower_half], axis=1).astype(jnp.bfloat16)


def polyphase(voltage, fir_taps):
    length = fir_taps.shape[1]
    window = voltage.reshape(voltage.shape[0], voltage.shape[1], -1, length)
    summed = jnp.zeros((voltage.shape[0], voltage.shape[1], SPEC, length), jnp.float32)
    for tap_index in range(TAPS):
        summed = summed + window[:, :, tap_index : tap_index + SPEC, :].astype(
            jnp.float32
        ) * fir_taps[tap_index].astype(jnp.float32)
    return summed.astype(jnp.bfloat16)


LANES = 128
STEP = 8
HALF = 16


def channelise_kernel(volt_ref, taps_ref, table_ref, gain_ref, out_ref, power_ref, cross_ref, filt, spec):
    length = taps_ref.shape[2]
    in_dev = volt_ref.shape[1]
    st_dev = in_dev // 2
    row_blocks = in_dev // HALF
    lane_blocks = length // LANES
    power_ref[...] = jnp.zeros_like(power_ref)
    cross_ref[...] = jnp.zeros_like(cross_ref)

    @pl.loop(0, SPEC // STEP)
    def _(block):
        first = block * STEP

        @pl.loop(0, 2 * row_blocks * lane_blocks)
        def _(turn):
            part = turn // (row_blocks * lane_blocks)
            row = pl.multiple_of(turn // lane_blocks % row_blocks * HALF, HALF)
            lane = pl.multiple_of(turn % lane_blocks * LANES, LANES)
            sums = [[None, None] for _ in range(STEP)]
            taps = [taps_ref[t, :, pl.ds(lane, LANES)] for t in range(TAPS)]
            for window in range(STEP + TAPS - 1):
                start = pl.multiple_of((first + window) * length + lane, LANES)
                both = volt_ref[part, pl.ds(row, HALF), pl.ds(start, LANES)].astype(jnp.float32)
                for half in range(2):
                    value = both[half * 8 : half * 8 + 8]
                    for s in range(max(0, window - TAPS + 1), min(STEP, window + 1)):
                        term = value * taps[window - s]
                        sums[s][half] = term if sums[s][half] is None else sums[s][half] + term
            column = pl.multiple_of(part * length + lane, LANES)
            for s in range(STEP):
                filt[s, pl.ds(row, HALF), pl.ds(column, LANES)] = jnp.concatenate(
                    sums[s], axis=0
                ).astype(jnp.bfloat16)

        rows = filt[...].reshape(STEP * in_dev, 2 * length)
        for column in range(2 * lane_blocks):
            product = jnp.dot(
                rows,
                table_ref[:, column * LANES : (column + 1) * LANES],
                preferred_element_type=jnp.float32,
            )
            spec[column] = product.astype(jnp.bfloat16).astype(jnp.float32)

        chunk = lax.broadcasted_iota(jnp.int32, (HALF, LANES), 1) // AVG
        for j in range(lane_blocks):
            lanes = slice(j * LANES, (j + 1) * LANES)
            for h in range(st_dev // HALF):
                st_rows = slice(h * HALF, (h + 1) * HALF)
                gre0, gim0, gre1, gim1 = (gain_ref[n, st_rows, lanes] for n in range(4))
                reals, imags = [], []
                power0 = power_ref[0, st_rows, lanes]
                power1 = power_ref[1, st_rows, lanes]
                cross = cross_ref[st_rows, lanes]
                for s in range(STEP):
                    base = s * in_dev + h * 2 * HALF
                    re0 = spec[j, pl.ds(base, HALF, stride=2), :]
                    re1 = spec[j, pl.ds(base + 1, HALF, stride=2), :]
                    im0 = spec[lane_blocks + j, pl.ds(base, HALF, stride=2), :]
                    im1 = spec[lane_blocks + j, pl.ds(base + 1, HALF, stride=2), :]
                    power0 = power0 + (re0 * re0 + im0 * im0)
                    power1 = power1 + (re1 * re1 + im1 * im1)
                    cre0 = re0 * gre0 - im0 * gim0
                    cim0 = re0 * gim0 + im0 * gre0
                    cre1 = re1 * gre1 - im1 * gim1
                    cim1 = re1 * gim1 + im1 * gre1
                    cross = cross + (cre0 * cre1 + cim0 * cim1)
                    reals.append(cre0 + cre1)
                    imags.append(cim0 + cim1)
                power_ref[0, st_rows, lanes] = power0
                power_ref[1, st_rows, lanes] = power1
                cross_ref[st_rows, lanes] = cross
                for q, planes in enumerate((reals, imags)):
                    bit = 1
                    while bit < STEP:
                        keep = (chunk // bit) % 2 == 0
                        for s in range(STEP):
                            if s & bit:
                                continue
                            low, high = planes[s], planes[s + bit]
                            shift = bit * AVG
                            planes[s] = jnp.where(keep, low, pltpu.roll(high, shift, 1))
                            planes[s + bit] = jnp.where(keep, pltpu.roll(low, LANES - shift, 1), high)
                        bit *= 2
                    where = pl.ds(pl.multiple_of(block * LANES, LANES), LANES)
                    for d in range(STEP):
                        out_ref[j * STEP + d, q, st_rows, where] = planes[d].astype(jnp.bfloat16)


def image_kernel(data_ref, steer_ref, out_ref, even_ref, odd_ref, along, turned):
    stations, depth = data_ref.shape[1], data_ref.shape[2]
    along[:, :depth] = data_ref[0]
    along[:, depth:] = data_ref[1]
    turned[:, :depth] = data_ref[1]
    turned[:, depth:] = -data_ref[0]
    contract = (((1,), (1,)), ((), ()))
    tall = 256

    @pl.loop(0, stations // tall)
    def _(block):
        rows = pl.ds(pl.multiple_of(block * tall, tall), tall)
        even = lax.dot_general(along[rows, :], along[...], contract, preferred_element_type=jnp.float32)
        odd = lax.dot_general(turned[rows, :], along[...], contract, preferred_element_type=jnp.float32)
        row_ids = lax.broadcasted_iota(jnp.int32, (tall, stations), 0) + block * tall
        same = row_ids == lax.broadcasted_iota(jnp.int32, (tall, stations), 1)
        even_ref[rows, :] = jnp.where(same, 0.0, even).astype(jnp.bfloat16)
        odd_ref[rows, :] = jnp.where(same, 0.0, -2.0 * odd).astype(jnp.bfloat16)

    tile = out_ref.shape[1]
    lines = tile // SIDE

    @pl.loop(0, out_ref.shape[0])
    def _(block):
        cosines, sines = [], []
        for line in range(lines):
            u = block * lines + line
            east_cos = steer_ref[0, pl.ds(u, 1), :]
            east_sin = steer_ref[1, pl.ds(u, 1), :]
            cosines.append(east_cos * steer_ref[2] - east_sin * steer_ref[3])
            sines.append(east_sin * steer_ref[2] + east_cos * steer_ref[3])
        cosine = jnp.concatenate(cosines, axis=0)
        sine = jnp.concatenate(sines, axis=0)
        cos16, sin16 = cosine.astype(jnp.bfloat16), sine.astype(jnp.bfloat16)
        first = jnp.dot(cos16, even_ref[...], preferred_element_type=jnp.float32)
        first = first + jnp.dot(sin16, odd_ref[...], preferred_element_type=jnp.float32)
        second = jnp.dot(sin16, even_ref[...], preferred_element_type=jnp.float32)
        terms = cosine * first + sine * second
        folded = terms[:, :LANES]
        for j in range(1, stations // LANES):
            folded = folded + terms[:, j * LANES : (j + 1) * LANES]
        out_ref[pl.ds(block, 1), :] = jnp.sum(folded.T, axis=0, keepdims=True)


def beam_images(joined, positions):
    steps = (jnp.arange(SIDE, dtype=jnp.float32) - SIDE // 2) / jnp.float32(SIDE)
    phases = jnp.float32(2.0 * math.pi) * (positions[:, None, :] * steps[None, :, None])
    steer = jnp.stack([jnp.cos(phases), jnp.sin(phases)], axis=1).reshape(
        4, SIDE, positions.shape[1]
    )
    stations, depth = joined.shape[1], joined.shape[2]
    vmem = pl.BlockSpec(memory_space=pltpu.VMEM)
    return pl.pallas_call(
        image_kernel,
        out_shape=jax.ShapeDtypeStruct((PIX // 256, 256), jnp.float32),
        in_specs=[vmem, vmem],
        out_specs=vmem,
        scratch_shapes=[
            pltpu.VMEM((stations, stations), jnp.bfloat16),
            pltpu.VMEM((stations, stations), jnp.bfloat16),
            pltpu.VMEM((stations, 2 * depth), jnp.bfloat16),
            pltpu.VMEM((stations, 2 * depth), jnp.bfloat16),
        ],
        compiler_params=pltpu.CompilerParams(vmem_limit_bytes=32 * 1024 * 1024),
        name="beam_images",
    )(joined, steer)


def channelise(voltages, fir_taps, gain_re, gain_im):
    in_dev = voltages.shape[1]
    st_dev = in_dev // 2
    table = jnp.transpose(dft_table(CH), (2, 3, 1, 0)).reshape(2 * CH, 2 * CH)
    taps = jnp.broadcast_to(fir_taps.astype(jnp.float32)[:, None], (TAPS, 8, CH))
    both = jnp.stack([gain_re, gain_im]).reshape(2, GROUPS, st_dev, 2)
    gains = jnp.repeat(jnp.transpose(both, (3, 0, 2, 1)).reshape(4, st_dev, GROUPS), AVG, axis=2)
    vmem = pl.BlockSpec(memory_space=pltpu.VMEM)
    return pl.pallas_call(
        channelise_kernel,
        out_shape=[
            jax.ShapeDtypeStruct((GROUPS, 2, st_dev, AVG * SPEC), jnp.bfloat16),
            jax.ShapeDtypeStruct((2, st_dev, CH), jnp.float32),
            jax.ShapeDtypeStruct((st_dev, CH), jnp.float32),
        ],
        in_specs=[vmem] * 4,
        out_specs=[vmem] * 3,
        scratch_shapes=[
            pltpu.VMEM((STEP, in_dev, 2 * CH), jnp.bfloat16),
            pltpu.VMEM((2 * CH // LANES, STEP * in_dev, LANES), jnp.float32),
        ],
        compiler_params=pltpu.CompilerParams(vmem_limit_bytes=32 * 1024 * 1024),
        name="channelise",
    )(voltages, taps, table, gains)


def channelise_small(voltages, fir_taps, gain_re, gain_im, chan_dev):
    in_dev = voltages.shape[1]
    st_dev = in_dev // 2
    spectra = jnp.einsum(
        "qrk,cpqk->cpr",
        polyphase(voltages, fir_taps).reshape(2, in_dev * SPEC, CH),
        dft_table(CH),
        preferred_element_type=jnp.float32,
    ).astype(jnp.bfloat16)
    values = spectra.astype(jnp.float32).reshape(GROUPS, AVG, 2, st_dev, 2, SPEC)
    powers = jnp.sum(values * values, axis=(2, 5)).reshape(CH, st_dev, 2)
    gre = gain_re.reshape(GROUPS, 1, st_dev, 2, 1)
    gim = gain_im.reshape(GROUPS, 1, st_dev, 2, 1)
    cal_re = values[:, :, 0] * gre - values[:, :, 1] * gim
    cal_im = values[:, :, 0] * gim + values[:, :, 1] * gre
    sums = jnp.stack(
        [cal_re[:, :, :, 0] + cal_re[:, :, :, 1], cal_im[:, :, :, 0] + cal_im[:, :, :, 1]]
    ).astype(jnp.bfloat16)
    crossed = cal_re[:, :, :, 0] * cal_re[:, :, :, 1] + cal_im[:, :, :, 0] * cal_im[:, :, :, 1]
    cross = jnp.sum(crossed, axis=3).reshape(CH, st_dev).T
    sums = jnp.transpose(
        sums.reshape(2, CH // chan_dev, chan_dev, st_dev, SPEC), (1, 0, 3, 2, 4)
    ).reshape(CH // chan_dev, 2, st_dev, chan_dev * SPEC)
    return sums, jnp.transpose(powers, (2, 1, 0)), cross


def local(voltages, fir_taps, positions, cal_amp, cal_phase, cal_index, owner_counts, tile_owner):
    devices = lax.axis_size("chan")
    myself = lax.axis_index("chan")
    in_dev = voltages.shape[1]
    st_dev = in_dev // 2
    stations = st_dev * devices
    chan_dev = CH // devices
    per_group = AVG // chan_dev

    my_index = lax.dynamic_slice_in_dim(cal_index, myself * in_dev, in_dev, 0)
    selection = (my_index[:, None] == jnp.arange(NCAL, dtype=jnp.int32)[None, :]).astype(jnp.float32)
    gain_re = jnp.dot(selection, cal_amp * jnp.cos(cal_phase), precision=highest).T
    gain_im = jnp.dot(selection, cal_amp * jnp.sin(cal_phase), precision=highest).T

    if chan_dev == AVG and st_dev % HALF == 0:
        outgoing, powers, crosses = channelise(voltages, fir_taps, gain_re, gain_im)
    else:
        outgoing, powers, crosses = channelise_small(voltages, fir_taps, gain_re, gain_im, chan_dev)
    incoming = lax.all_to_all(outgoing, "chan", split_axis=0, concat_axis=0, tiled=True)


    power_rows = jnp.transpose(powers, (2, 1, 0)).reshape(CH, in_dev) / jnp.float32(SPEC)
    offsets = jnp.cumsum(owner_counts) - owner_counts
    chan_ids = jnp.arange(CH, dtype=jnp.int32)
    member = (
        (chan_ids[None, :] >= offsets[:, None])
        & (chan_ids[None, :] < (offsets + owner_counts)[:, None])
    ).astype(jnp.float32)
    divisor = jnp.maximum(owner_counts, 1).astype(jnp.float32)
    sub_rows = jnp.dot(member, power_rows, precision=highest) / divisor[:, None]

    cross_power = 2.0 * jnp.sum(crosses.reshape(st_dev, GROUPS, AVG), axis=(0, 2))
    joined = jnp.transpose(incoming, (1, 0, 2, 3)).reshape(2, stations, chan_dev * SPEC)
    image = beam_images(joined, positions)

    tile_pix = PIX // devices
    device_ids = jnp.arange(devices, dtype=jnp.int32)
    tile_of = jnp.sum(
        jnp.where(tile_owner[None, :] == device_ids[:, None], device_ids[None, :], 0), axis=1
    )
    tiles = image.reshape(devices, tile_pix)[tile_of]
    last = jnp.concatenate(
        [tiles, sub_rows, jnp.broadcast_to(cross_power[None], (devices, GROUPS))], axis=1
    )
    arrived = lax.all_to_all(last, "chan", split_axis=0, concat_axis=0, tiled=True)
    scale = jnp.float32(1.0 / (SPEC * AVG) * math.sqrt(SPEC * AVG) / (2 * stations))
    pieces = jnp.sum(arrived[:, :tile_pix].reshape(GROUPS, per_group, tile_pix), axis=1)
    constant = jnp.sum(arrived[:, tile_pix + in_dev :], axis=0)
    result = scale * (pieces + constant[:, None])
    autos = arrived[:, tile_pix : tile_pix + in_dev].reshape(1, devices * in_dev)
    return (result[None], autos)


def solution(mesh):
    in_specs = (
        P(None, ("grp", "chan"), None),
        P(),
        P(),
        P("grp", None),
        P("grp", None),
        P(),
        P("grp"),
        P("grp"),
    )
    out_specs = (P(("grp", "chan"), None, None), P(("grp", "chan"), None))
    return jax.shard_map(local, mesh=mesh, in_specs=in_specs, out_specs=out_specs, check_vma=False)
```

```python
import math

import jax
import numpy as np
import jax.numpy as jnp
from jax import lax
from jax.experimental import pallas as pl
from jax.experimental.pallas import tpu as pltpu
from jax.sharding import PartitionSpec as P

CH = 256
AVG = 16
GROUPS = 16
SPEC = 32
TAPS = 16
SIDE = 64
PIX = 4096
NCAL = 256

highest = lax.Precision.HIGHEST


def dft_table(length):
    indices = np.arange(length, dtype=np.int64)
    angles = (indices[:, None] * indices[None, :] % length) * (2.0 * math.pi / length)
    cosine = np.cos(angles) / math.sqrt(length)
    sine_part = np.sin(angles) / math.sqrt(length)
    upper_half = np.stack([cosine, sine_part], axis=1)
    lower_half = np.stack([-sine_part, cosine], axis=1)
    return np.stack([upper_half, lower_half], axis=1).astype(jnp.bfloat16)


def polyphase(voltage, fir_taps):
    length = fir_taps.shape[1]
    window = voltage.reshape(voltage.shape[0], voltage.shape[1], -1, length)
    summed = jnp.zeros((voltage.shape[0], voltage.shape[1], SPEC, length), jnp.float32)
    for tap_index in range(TAPS):
        summed = summed + window[:, :, tap_index : tap_index + SPEC, :].astype(
            jnp.float32
        ) * fir_taps[tap_index].astype(jnp.float32)
    return summed.astype(jnp.bfloat16)


LANES = 128
STEP = 8
HALF = 16


def channelise_kernel(
    volt_ref, fir_ref, table_ref, index_ref, solution_ref, out_ref, power_ref, cross_ref,
    filt, spec, taps_ref, gain_ref,
):
    length = fir_ref.shape[1]
    in_dev = volt_ref.shape[1]
    st_dev = in_dev // 2
    row_blocks = in_dev // HALF
    lane_blocks = length // LANES
    power_ref[...] = jnp.zeros_like(power_ref)
    cross_ref[...] = jnp.zeros_like(cross_ref)
    fir = fir_ref[...].astype(jnp.float32)
    for t in range(TAPS):
        taps_ref[t] = jnp.broadcast_to(fir[t : t + 1], (8, length))
    group_ids = lax.broadcasted_iota(jnp.int32, (GROUPS, length), 0)
    spread = (
        group_ids == lax.broadcasted_iota(jnp.int32, (GROUPS, length), 1) // AVG
    ).astype(jnp.float32)
    solution_ids = lax.broadcasted_iota(jnp.int32, (NCAL, st_dev), 0)
    for pol in range(2):
        chosen = (solution_ids == index_ref[pol : pol + 1, :]).astype(jnp.float32)
        for q in range(2):
            picked = lax.dot_general(
                chosen,
                solution_ref[q],
                (((0,), (0,)), ((), ())),
                precision=highest,
                preferred_element_type=jnp.float32,
            )
            gain_ref[pol * 2 + q] = jnp.dot(
                picked, spread, precision=highest, preferred_element_type=jnp.float32
            )

    @pl.loop(0, SPEC // STEP)
    def _(block):
        first = block * STEP

        @pl.loop(0, 2 * row_blocks * lane_blocks)
        def _(turn):
            part = turn // (row_blocks * lane_blocks)
            row = pl.multiple_of(turn // lane_blocks % row_blocks * HALF, HALF)
            lane = pl.multiple_of(turn % lane_blocks * LANES, LANES)
            sums = [[None, None] for _ in range(STEP)]
            taps = [taps_ref[t, :, pl.ds(lane, LANES)] for t in range(TAPS)]
            for window in range(STEP + TAPS - 1):
                start = pl.multiple_of((first + window) * length + lane, LANES)
                both = volt_ref[part, pl.ds(row, HALF), pl.ds(start, LANES)].astype(jnp.float32)
                for half in range(2):
                    value = both[half * 8 : half * 8 + 8]
                    for s in range(max(0, window - TAPS + 1), min(STEP, window + 1)):
                        term = value * taps[window - s]
                        sums[s][half] = term if sums[s][half] is None else sums[s][half] + term
            column = pl.multiple_of(part * length + lane, LANES)
            for s in range(STEP):
                filt[s, pl.ds(row, HALF), pl.ds(column, LANES)] = jnp.concatenate(
                    sums[s], axis=0
                ).astype(jnp.bfloat16)

        rows = filt[...].reshape(STEP * in_dev, 2 * length)
        for column in range(2 * lane_blocks):
            product = jnp.dot(
                rows,
                table_ref[:, column * LANES : (column + 1) * LANES],
                preferred_element_type=jnp.float32,
            )
            spec[column] = product.astype(jnp.bfloat16).astype(jnp.float32)

        chunk = lax.broadcasted_iota(jnp.int32, (HALF, LANES), 1) // AVG
        for j in range(lane_blocks):
            lanes = slice(j * LANES, (j + 1) * LANES)
            for h in range(st_dev // HALF):
                st_rows = slice(h * HALF, (h + 1) * HALF)
                gre0, gim0, gre1, gim1 = (gain_ref[n, st_rows, lanes] for n in range(4))
                reals, imags = [], []
                power0 = power_ref[0, st_rows, lanes]
                power1 = power_ref[1, st_rows, lanes]
                cross = cross_ref[st_rows, lanes]
                for s in range(STEP):
                    base = s * in_dev + h * 2 * HALF
                    re0 = spec[j, pl.ds(base, HALF, stride=2), :]
                    re1 = spec[j, pl.ds(base + 1, HALF, stride=2), :]
                    im0 = spec[lane_blocks + j, pl.ds(base, HALF, stride=2), :]
                    im1 = spec[lane_blocks + j, pl.ds(base + 1, HALF, stride=2), :]
                    power0 = power0 + (re0 * re0 + im0 * im0)
                    power1 = power1 + (re1 * re1 + im1 * im1)
                    cre0 = re0 * gre0 - im0 * gim0
                    cim0 = re0 * gim0 + im0 * gre0
                    cre1 = re1 * gre1 - im1 * gim1
                    cim1 = re1 * gim1 + im1 * gre1
                    cross = cross + (cre0 * cre1 + cim0 * cim1)
                    reals.append(cre0 + cre1)
                    imags.append(cim0 + cim1)
                power_ref[0, st_rows, lanes] = power0
                power_ref[1, st_rows, lanes] = power1
                cross_ref[st_rows, lanes] = cross
                for q, planes in enumerate((reals, imags)):
                    bit = 1
                    while bit < STEP:
                        keep = (chunk // bit) % 2 == 0
                        for s in range(STEP):
                            if s & bit:
                                continue
                            low, high = planes[s], planes[s + bit]
                            shift = bit * AVG
                            planes[s] = jnp.where(keep, low, pltpu.roll(high, shift, 1))
                            planes[s + bit] = jnp.where(keep, pltpu.roll(low, LANES - shift, 1), high)
                        bit *= 2
                    where = pl.ds(pl.multiple_of(block * LANES, LANES), LANES)
                    for d in range(STEP):
                        out_ref[j * STEP + d, q, st_rows, where] = planes[d].astype(jnp.bfloat16)


def image_kernel(data_ref, steer_ref, out_ref, even_ref, odd_ref, along, turned):
    stations, depth = data_ref.shape[1], data_ref.shape[2]
    along[:, :depth] = data_ref[0]
    along[:, depth:] = data_ref[1]
    turned[:, :depth] = data_ref[1]
    turned[:, depth:] = -data_ref[0]
    contract = (((1,), (1,)), ((), ()))
    tall = 256

    @pl.loop(0, stations // tall)
    def _(block):
        rows = pl.ds(pl.multiple_of(block * tall, tall), tall)
        even = lax.dot_general(along[rows, :], along[...], contract, preferred_element_type=jnp.float32)
        odd = lax.dot_general(turned[rows, :], along[...], contract, preferred_element_type=jnp.float32)
        row_ids = lax.broadcasted_iota(jnp.int32, (tall, stations), 0) + block * tall
        same = row_ids == lax.broadcasted_iota(jnp.int32, (tall, stations), 1)
        even_ref[rows, :] = jnp.where(same, 0.0, even).astype(jnp.bfloat16)
        odd_ref[rows, :] = jnp.where(same, 0.0, -2.0 * odd).astype(jnp.bfloat16)

    tile = out_ref.shape[1]

    @pl.loop(0, out_ref.shape[0], unroll=2)
    def _(block):
        pixels = pl.ds(pl.multiple_of(block * tile, tile), tile)
        cosine, sine = steer_ref[0, pixels, :], steer_ref[1, pixels, :]
        cos16, sin16 = cosine.astype(jnp.bfloat16), sine.astype(jnp.bfloat16)
        first = jnp.dot(cos16, even_ref[...], preferred_element_type=jnp.float32)
        first = first + jnp.dot(sin16, odd_ref[...], preferred_element_type=jnp.float32)
        second = jnp.dot(sin16, even_ref[...], preferred_element_type=jnp.float32)
        terms = cosine * first + sine * second
        folded = terms[:, :LANES]
        for j in range(1, stations // LANES):
            folded = folded + terms[:, j * LANES : (j + 1) * LANES]
        out_ref[pl.ds(block, 1), :] = jnp.sum(folded.T, axis=0, keepdims=True)


def steering_kernel(axis_ref, out_ref):
    @pl.loop(0, SIDE)
    def _(u):
        east_cos = axis_ref[0, pl.ds(u, 1), :]
        east_sin = axis_ref[1, pl.ds(u, 1), :]
        pixels = pl.ds(pl.multiple_of(u * SIDE, SIDE), SIDE)
        out_ref[0, pixels, :] = east_cos * axis_ref[2] - east_sin * axis_ref[3]
        out_ref[1, pixels, :] = east_sin * axis_ref[2] + east_cos * axis_ref[3]


def steering_tables(positions):
    steps = (jnp.arange(SIDE, dtype=jnp.float32) - SIDE // 2) / jnp.float32(SIDE)
    phases = jnp.float32(2.0 * math.pi) * (positions[:, None, :] * steps[None, :, None])
    stations = positions.shape[1]
    axes = jnp.stack([jnp.cos(phases), jnp.sin(phases)], axis=1).reshape(4, SIDE, stations)
    vmem = pl.BlockSpec(memory_space=pltpu.VMEM)
    return pl.pallas_call(
        steering_kernel,
        out_shape=jax.ShapeDtypeStruct((2, PIX, stations), jnp.float32),
        in_specs=[vmem],
        out_specs=vmem,
        cost_estimate=pl.CostEstimate(
            flops=6 * PIX * stations, bytes_accessed=8 * PIX * stations, transcendentals=0
        ),
        compiler_params=pltpu.CompilerParams(vmem_limit_bytes=24 * 1024 * 1024),
        name="steering",
    )(axes)


def beam_images(joined, steer):
    stations, depth = joined.shape[1], joined.shape[2]
    vmem = pl.BlockSpec(memory_space=pltpu.VMEM)
    return pl.pallas_call(
        image_kernel,
        out_shape=jax.ShapeDtypeStruct((PIX // 256, 256), jnp.float32),
        in_specs=[vmem, vmem],
        out_specs=vmem,
        scratch_shapes=[
            pltpu.VMEM((stations, stations), jnp.bfloat16),
            pltpu.VMEM((stations, stations), jnp.bfloat16),
            pltpu.VMEM((stations, 2 * depth), jnp.bfloat16),
            pltpu.VMEM((stations, 2 * depth), jnp.bfloat16),
        ],
        compiler_params=pltpu.CompilerParams(vmem_limit_bytes=36 * 1024 * 1024),
        name="beam_images",
    )(joined, steer)


def channelise(voltages, fir_taps, my_index, solutions):
    in_dev = voltages.shape[1]
    st_dev = in_dev // 2
    table = jnp.asarray(np.transpose(dft_table(CH), (2, 3, 1, 0)).reshape(2 * CH, 2 * CH))
    vmem = pl.BlockSpec(memory_space=pltpu.VMEM)
    return pl.pallas_call(
        channelise_kernel,
        out_shape=[
            jax.ShapeDtypeStruct((GROUPS, 2, st_dev, AVG * SPEC), jnp.bfloat16),
            jax.ShapeDtypeStruct((2, st_dev, CH), jnp.float32),
            jax.ShapeDtypeStruct((st_dev, CH), jnp.float32),
        ],
        in_specs=[vmem] * 5,
        out_specs=[vmem] * 3,
        scratch_shapes=[
            pltpu.VMEM((STEP, in_dev, 2 * CH), jnp.bfloat16),
            pltpu.VMEM((2 * CH // LANES, STEP * in_dev, LANES), jnp.float32),
            pltpu.VMEM((TAPS, 8, CH), jnp.float32),
            pltpu.VMEM((4, st_dev, CH), jnp.float32),
        ],
        compiler_params=pltpu.CompilerParams(vmem_limit_bytes=32 * 1024 * 1024),
        name="channelise",
    )(voltages, fir_taps, table, my_index, solutions)


def channelise_small(voltages, fir_taps, my_index, solutions, chan_dev):
    in_dev = voltages.shape[1]
    st_dev = in_dev // 2
    spectra = jnp.einsum(
        "qrk,cpqk->cpr",
        polyphase(voltages, fir_taps).reshape(2, in_dev * SPEC, CH),
        dft_table(CH),
        preferred_element_type=jnp.float32,
    ).astype(jnp.bfloat16)
    values = spectra.astype(jnp.float32).reshape(GROUPS, AVG, 2, st_dev, 2, SPEC)
    powers = jnp.sum(values * values, axis=(2, 5)).reshape(CH, st_dev, 2)
    selection = (my_index.T[..., None] == jnp.arange(NCAL, dtype=jnp.int32)).astype(jnp.float32)
    gains = jnp.einsum("kpn,qng->qgkp", selection, solutions, precision=highest)
    gre, gim = gains[:, :, None, :, :, None]
    cal_re = values[:, :, 0] * gre - values[:, :, 1] * gim
    cal_im = values[:, :, 0] * gim + values[:, :, 1] * gre
    sums = jnp.stack(
        [cal_re[:, :, :, 0] + cal_re[:, :, :, 1], cal_im[:, :, :, 0] + cal_im[:, :, :, 1]]
    ).astype(jnp.bfloat16)
    crossed = cal_re[:, :, :, 0] * cal_re[:, :, :, 1] + cal_im[:, :, :, 0] * cal_im[:, :, :, 1]
    cross = jnp.sum(crossed, axis=3).reshape(CH, st_dev).T
    sums = jnp.transpose(
        sums.reshape(2, CH // chan_dev, chan_dev, st_dev, SPEC), (1, 0, 3, 2, 4)
    ).reshape(CH // chan_dev, 2, st_dev, chan_dev * SPEC)
    return sums, jnp.transpose(powers, (2, 1, 0)), cross


def local(voltages, fir_taps, positions, cal_amp, cal_phase, cal_index, owner_counts, tile_owner):
    devices = lax.axis_size("chan")
    myself = lax.axis_index("chan")
    in_dev = voltages.shape[1]
    st_dev = in_dev // 2
    stations = st_dev * devices
    chan_dev = CH // devices
    per_group = AVG // chan_dev

    solutions = jnp.stack([cal_amp * jnp.cos(cal_phase), cal_amp * jnp.sin(cal_phase)])
    my_index = lax.dynamic_slice_in_dim(cal_index, myself * in_dev, in_dev, 0)
    my_index = my_index.reshape(st_dev, 2).T
    if chan_dev == AVG and st_dev % HALF == 0:
        outgoing, powers, crosses = channelise(voltages, fir_taps, my_index, solutions)
    else:
        outgoing, powers, crosses = channelise_small(voltages, fir_taps, my_index, solutions, chan_dev)
    incoming = lax.all_to_all(outgoing, "chan", split_axis=0, concat_axis=0, tiled=True)


    power_rows = jnp.transpose(powers, (2, 1, 0)).reshape(CH, in_dev) / jnp.float32(SPEC)
    offsets = jnp.cumsum(owner_counts) - owner_counts
    chan_ids = jnp.arange(CH, dtype=jnp.int32)
    member = (
        (chan_ids[None, :] >= offsets[:, None])
        & (chan_ids[None, :] < (offsets + owner_counts)[:, None])
    ).astype(jnp.float32)
    divisor = jnp.maximum(owner_counts, 1).astype(jnp.float32)
    sub_rows = jnp.dot(member, power_rows, precision=highest) / divisor[:, None]

    cross_power = 2.0 * jnp.sum(crosses.reshape(st_dev, GROUPS, AVG), axis=(0, 2))
    joined = jnp.transpose(incoming, (1, 0, 2, 3)).reshape(2, stations, chan_dev * SPEC)
    image = beam_images(joined, steering_tables(positions))

    tile_pix = PIX // devices
    device_ids = jnp.arange(devices, dtype=jnp.int32)
    tile_of = jnp.sum(
        jnp.where(tile_owner[None, :] == device_ids[:, None], device_ids[None, :], 0), axis=1
    )
    tiles = image.reshape(devices, tile_pix)[tile_of]
    last = jnp.concatenate(
        [tiles, sub_rows, jnp.broadcast_to(cross_power[None], (devices, GROUPS))], axis=1
    )
    arrived = lax.all_to_all(last, "chan", split_axis=0, concat_axis=0, tiled=True)
    scale = jnp.float32(1.0 / (SPEC * AVG) * math.sqrt(SPEC * AVG) / (2 * stations))
    pieces = jnp.sum(arrived[:, :tile_pix].reshape(GROUPS, per_group, tile_pix), axis=1)
    constant = jnp.sum(arrived[:, tile_pix + in_dev :], axis=0)
    result = scale * (pieces + constant[:, None])
    autos = arrived[:, tile_pix : tile_pix + in_dev].reshape(1, devices * in_dev)
    return (result[None], autos)


def solution(mesh):
    in_specs = (
        P(None, ("grp", "chan"), None),
        P(),
        P(),
        P("grp", None),
        P("grp", None),
        P(),
        P("grp"),
        P("grp"),
    )
    out_specs = (P(("grp", "chan"), None, None), P(("grp", "chan"), None))
    return jax.shard_map(local, mesh=mesh, in_specs=in_specs, out_specs=out_specs, check_vma=False)
```

```python
import math

import jax
import numpy as np
import jax.numpy as jnp
from jax import lax
from jax.experimental import pallas as pl
from jax.experimental.pallas import tpu as pltpu
from jax.sharding import PartitionSpec as P

CH = 256
AVG = 16
GROUPS = 16
SPEC = 32
TAPS = 16
SIDE = 64
PIX = 4096
NCAL = 256

highest = lax.Precision.HIGHEST


def dft_table(length):
    indices = np.arange(length, dtype=np.int64)
    angles = (indices[:, None] * indices[None, :] % length) * (2.0 * math.pi / length)
    cosine = np.cos(angles) / math.sqrt(length)
    sine_part = np.sin(angles) / math.sqrt(length)
    upper_half = np.stack([cosine, sine_part], axis=1)
    lower_half = np.stack([-sine_part, cosine], axis=1)
    return np.stack([upper_half, lower_half], axis=1).astype(jnp.bfloat16)


def polyphase(voltage, fir_taps):
    length = fir_taps.shape[1]
    window = voltage.reshape(voltage.shape[0], voltage.shape[1], -1, length)
    summed = jnp.zeros((voltage.shape[0], voltage.shape[1], SPEC, length), jnp.float32)
    for tap_index in range(TAPS):
        summed = summed + window[:, :, tap_index : tap_index + SPEC, :].astype(
            jnp.float32
        ) * fir_taps[tap_index].astype(jnp.float32)
    return summed.astype(jnp.bfloat16)


LANES = 128
STEP = 8
HALF = 16


def channelise_kernel(
    volt_ref, fir_ref, table_ref, index_ref, solution_ref, out_ref, power_ref, cross_ref,
    filt, spec, taps_ref, gain_ref,
):
    length = fir_ref.shape[1]
    in_dev = volt_ref.shape[1]
    st_dev = in_dev // 2
    row_blocks = in_dev // HALF
    lane_blocks = length // LANES
    power_ref[...] = jnp.zeros_like(power_ref)
    cross_ref[...] = jnp.zeros_like(cross_ref)
    fir = fir_ref[...].astype(jnp.float32)
    for t in range(TAPS):
        taps_ref[t] = jnp.broadcast_to(fir[t : t + 1], (8, length))
    chosen = (
        lax.broadcasted_iota(jnp.int32, (NCAL, in_dev), 0) == index_ref[...]
    ).astype(jnp.float32)
    picked = lax.dot_general(
        chosen,
        solution_ref[...],
        (((0,), (0,)), ((), ())),
        precision=highest,
        preferred_element_type=jnp.float32,
    )
    column_ids = lax.broadcasted_iota(jnp.int32, (2 * GROUPS, length), 0)
    group_ids = lax.broadcasted_iota(jnp.int32, (2 * GROUPS, length), 1) // AVG
    for q in range(2):
        spread = (column_ids == group_ids + q * GROUPS).astype(jnp.float32)
        gains = jnp.dot(picked, spread, precision=highest, preferred_element_type=jnp.float32)
        gain_ref[q] = gains[:st_dev]
        gain_ref[2 + q] = gains[st_dev:]

    @pl.loop(0, SPEC // STEP)
    def _(block):
        first = block * STEP

        @pl.loop(0, 2 * row_blocks * lane_blocks)
        def _(turn):
            part = turn // (row_blocks * lane_blocks)
            row = pl.multiple_of(turn // lane_blocks % row_blocks * HALF, HALF)
            lane = pl.multiple_of(turn % lane_blocks * LANES, LANES)
            sums = [[None, None] for _ in range(STEP)]
            taps = [taps_ref[t, :, pl.ds(lane, LANES)] for t in range(TAPS)]
            for window in range(STEP + TAPS - 1):
                start = pl.multiple_of((first + window) * length + lane, LANES)
                both = volt_ref[part, pl.ds(row, HALF), pl.ds(start, LANES)].astype(jnp.float32)
                for half in range(2):
                    value = both[half * 8 : half * 8 + 8]
                    for s in range(max(0, window - TAPS + 1), min(STEP, window + 1)):
                        term = value * taps[window - s]
                        sums[s][half] = term if sums[s][half] is None else sums[s][half] + term
            column = pl.multiple_of(part * length + lane, LANES)
            for s in range(STEP):
                filt[s, pl.ds(row, HALF), pl.ds(column, LANES)] = jnp.concatenate(
                    sums[s], axis=0
                ).astype(jnp.bfloat16)

        rows = filt[...].reshape(STEP * in_dev, 2 * length)
        for column in range(2 * lane_blocks):
            product = jnp.dot(
                rows,
                table_ref[:, column * LANES : (column + 1) * LANES],
                preferred_element_type=jnp.float32,
            )
            spec[column] = product.astype(jnp.bfloat16).astype(jnp.float32)

        chunk = lax.broadcasted_iota(jnp.int32, (HALF, LANES), 1) // AVG
        for j in range(lane_blocks):
            lanes = slice(j * LANES, (j + 1) * LANES)
            for h in range(st_dev // HALF):
                st_rows = slice(h * HALF, (h + 1) * HALF)
                gre0, gim0, gre1, gim1 = (gain_ref[n, st_rows, lanes] for n in range(4))
                reals, imags = [], []
                power0 = power_ref[0, st_rows, lanes]
                power1 = power_ref[1, st_rows, lanes]
                cross = cross_ref[st_rows, lanes]
                for s in range(STEP):
                    base = s * in_dev + h * 2 * HALF
                    re0 = spec[j, pl.ds(base, HALF, stride=2), :]
                    re1 = spec[j, pl.ds(base + 1, HALF, stride=2), :]
                    im0 = spec[lane_blocks + j, pl.ds(base, HALF, stride=2), :]
                    im1 = spec[lane_blocks + j, pl.ds(base + 1, HALF, stride=2), :]
                    power0 = power0 + (re0 * re0 + im0 * im0)
                    power1 = power1 + (re1 * re1 + im1 * im1)
                    cre0 = re0 * gre0 - im0 * gim0
                    cim0 = re0 * gim0 + im0 * gre0
                    cre1 = re1 * gre1 - im1 * gim1
                    cim1 = re1 * gim1 + im1 * gre1
                    cross = cross + (cre0 * cre1 + cim0 * cim1)
                    reals.append(cre0 + cre1)
                    imags.append(cim0 + cim1)
                power_ref[0, st_rows, lanes] = power0
                power_ref[1, st_rows, lanes] = power1
                cross_ref[st_rows, lanes] = cross
                for q, planes in enumerate((reals, imags)):
                    bit = 1
                    while bit < STEP:
                        keep = (chunk // bit) % 2 == 0
                        for s in range(STEP):
                            if s & bit:
                                continue
                            low, high = planes[s], planes[s + bit]
                            shift = bit * AVG
                            planes[s] = jnp.where(keep, low, pltpu.roll(high, shift, 1))
                            planes[s + bit] = jnp.where(keep, pltpu.roll(low, LANES - shift, 1), high)
                        bit *= 2
                    where = pl.ds(pl.multiple_of(block * LANES, LANES), LANES)
                    for d in range(STEP):
                        out_ref[j * STEP + d, q, st_rows, where] = planes[d].astype(jnp.bfloat16)


def image_kernel(data_ref, steer_ref, out_ref, even_ref, odd_ref, along, turned):
    stations, depth = data_ref.shape[1], data_ref.shape[2]
    along[:, :depth] = data_ref[0]
    along[:, depth:] = data_ref[1]
    turned[:, :depth] = data_ref[1]
    turned[:, depth:] = -data_ref[0]
    contract = (((1,), (1,)), ((), ()))
    tall = 256

    @pl.loop(0, stations // tall)
    def _(block):
        rows = pl.ds(pl.multiple_of(block * tall, tall), tall)
        even = lax.dot_general(along[rows, :], along[...], contract, preferred_element_type=jnp.float32)
        odd = lax.dot_general(turned[rows, :], along[...], contract, preferred_element_type=jnp.float32)
        row_ids = lax.broadcasted_iota(jnp.int32, (tall, stations), 0) + block * tall
        same = row_ids == lax.broadcasted_iota(jnp.int32, (tall, stations), 1)
        even_ref[rows, :] = jnp.where(same, 0.0, even).astype(jnp.bfloat16)
        odd_ref[rows, :] = jnp.where(same, 0.0, -2.0 * odd).astype(jnp.bfloat16)

    tile = out_ref.shape[1]
    lines = tile // SIDE

    @pl.loop(0, out_ref.shape[0], unroll=4)
    def _(block):
        cosines, sines = [], []
        for line in range(lines):
            u = block * lines + line
            east_cos = steer_ref[0, pl.ds(u, 1), :]
            east_sin = steer_ref[1, pl.ds(u, 1), :]
            cosines.append(east_cos * steer_ref[2] - east_sin * steer_ref[3])
            sines.append(east_sin * steer_ref[2] + east_cos * steer_ref[3])
        cosine = jnp.concatenate(cosines, axis=0)
        sine = jnp.concatenate(sines, axis=0)
        cos16, sin16 = cosine.astype(jnp.bfloat16), sine.astype(jnp.bfloat16)
        first = jnp.dot(cos16, even_ref[...], preferred_element_type=jnp.float32)
        first = first + jnp.dot(sin16, odd_ref[...], preferred_element_type=jnp.float32)
        second = jnp.dot(sin16, even_ref[...], preferred_element_type=jnp.float32)
        terms = cosine * first + sine * second
        folded = terms[:, :LANES]
        for j in range(1, stations // LANES):
            folded = folded + terms[:, j * LANES : (j + 1) * LANES]
        out_ref[pl.ds(block, 1), :] = jnp.sum(folded.T, axis=0, keepdims=True)


def exchange_kernel(source_ref, target_ref, sent, landed, own):
    count = source_ref.shape[0]
    me = lax.axis_index("chan")
    barrier = pltpu.get_barrier_semaphore()

    @pl.loop(1, count)
    def _(step):
        pl.semaphore_signal(
            barrier,
            inc=1,
            device_id={"chan": lax.rem(me + step, count)},
            device_id_type=pl.DeviceIdType.MESH,
        )

    local_copy = pltpu.make_async_copy(source_ref.at[me], target_ref.at[me], own)
    local_copy.start()
    pl.semaphore_wait(barrier, count - 1)

    def transfer(step, slot):
        peer = lax.rem(me + step, count)
        return pltpu.make_async_remote_copy(
            src_ref=source_ref.at[peer],
            dst_ref=target_ref.at[slot],
            send_sem=sent.at[step],
            recv_sem=landed.at[step],
            device_id={"chan": peer},
            device_id_type=pl.DeviceIdType.MESH,
        )

    @pl.loop(1, count)
    def _(step):
        transfer(step, me).start()

    local_copy.wait()

    @pl.loop(1, count)
    def _(step):
        transfer(step, lax.rem(me + count - step, count)).wait()


def exchange(blocks, number):
    count = blocks.shape[0]
    if count > 16:
        return lax.all_to_all(blocks, "chan", split_axis=0, concat_axis=0, tiled=True)
    vmem = pl.BlockSpec(memory_space=pltpu.VMEM)
    return pl.pallas_call(
        exchange_kernel,
        out_shape=jax.ShapeDtypeStruct(blocks.shape, blocks.dtype),
        in_specs=[vmem],
        out_specs=vmem,
        scratch_shapes=[
            pltpu.SemaphoreType.DMA((count,)),
            pltpu.SemaphoreType.DMA((count,)),
            pltpu.SemaphoreType.DMA,
        ],
        compiler_params=pltpu.CompilerParams(
            collective_id=number, has_side_effects=True, vmem_limit_bytes=16 * 1024 * 1024
        ),
        name="exchange",
    )(blocks)


def steering_axes(positions):
    steps = (jnp.arange(SIDE, dtype=jnp.float32) - SIDE // 2) / jnp.float32(SIDE)
    phases = jnp.float32(2.0 * math.pi) * (positions[:, None, :] * steps[None, :, None])
    stations = positions.shape[1]
    return jnp.stack([jnp.cos(phases), jnp.sin(phases)], axis=1).reshape(4, SIDE, stations)


def beam_images(joined, steer):
    stations, depth = joined.shape[1], joined.shape[2]
    vmem = pl.BlockSpec(memory_space=pltpu.VMEM)
    return pl.pallas_call(
        image_kernel,
        out_shape=jax.ShapeDtypeStruct((PIX // 256, 256), jnp.float32),
        in_specs=[vmem, vmem],
        out_specs=vmem,
        scratch_shapes=[
            pltpu.VMEM((stations, stations), jnp.bfloat16),
            pltpu.VMEM((stations, stations), jnp.bfloat16),
            pltpu.VMEM((stations, 2 * depth), jnp.bfloat16),
            pltpu.VMEM((stations, 2 * depth), jnp.bfloat16),
        ],
        compiler_params=pltpu.CompilerParams(vmem_limit_bytes=36 * 1024 * 1024),
        name="beam_images",
    )(joined, steer)


def channelise(voltages, fir_taps, my_index, solutions):
    in_dev = voltages.shape[1]
    st_dev = in_dev // 2
    table = jnp.asarray(np.transpose(dft_table(CH), (2, 3, 1, 0)).reshape(2 * CH, 2 * CH))
    vmem = pl.BlockSpec(memory_space=pltpu.VMEM)
    return pl.pallas_call(
        channelise_kernel,
        out_shape=[
            jax.ShapeDtypeStruct((GROUPS, 2, st_dev, AVG * SPEC), jnp.bfloat16),
            jax.ShapeDtypeStruct((2, st_dev, CH), jnp.float32),
            jax.ShapeDtypeStruct((st_dev, CH), jnp.float32),
        ],
        in_specs=[vmem] * 5,
        out_specs=[vmem] * 3,
        scratch_shapes=[
            pltpu.VMEM((STEP, in_dev, 2 * CH), jnp.bfloat16),
            pltpu.VMEM((2 * CH // LANES, STEP * in_dev, LANES), jnp.float32),
            pltpu.VMEM((TAPS, 8, CH), jnp.float32),
            pltpu.VMEM((4, st_dev, CH), jnp.float32),
        ],
        compiler_params=pltpu.CompilerParams(vmem_limit_bytes=32 * 1024 * 1024),
        name="channelise",
    )(voltages, fir_taps, table, my_index, solutions)


def channelise_small(voltages, fir_taps, my_index, solutions, chan_dev):
    in_dev = voltages.shape[1]
    st_dev = in_dev // 2
    spectra = jnp.einsum(
        "qrk,cpqk->cpr",
        polyphase(voltages, fir_taps).reshape(2, in_dev * SPEC, CH),
        dft_table(CH),
        preferred_element_type=jnp.float32,
    ).astype(jnp.bfloat16)
    values = spectra.astype(jnp.float32).reshape(GROUPS, AVG, 2, st_dev, 2, SPEC)
    powers = jnp.sum(values * values, axis=(2, 5)).reshape(CH, st_dev, 2)
    selection = (my_index.T[..., None] == jnp.arange(NCAL, dtype=jnp.int32)).astype(jnp.float32)
    gains = jnp.einsum("kpn,qng->qgkp", selection, solutions, precision=highest)
    gre, gim = gains[:, :, None, :, :, None]
    cal_re = values[:, :, 0] * gre - values[:, :, 1] * gim
    cal_im = values[:, :, 0] * gim + values[:, :, 1] * gre
    sums = jnp.stack(
        [cal_re[:, :, :, 0] + cal_re[:, :, :, 1], cal_im[:, :, :, 0] + cal_im[:, :, :, 1]]
    ).astype(jnp.bfloat16)
    crossed = cal_re[:, :, :, 0] * cal_re[:, :, :, 1] + cal_im[:, :, :, 0] * cal_im[:, :, :, 1]
    cross = jnp.sum(crossed, axis=3).reshape(CH, st_dev).T
    sums = jnp.transpose(
        sums.reshape(2, CH // chan_dev, chan_dev, st_dev, SPEC), (1, 0, 3, 2, 4)
    ).reshape(CH // chan_dev, 2, st_dev, chan_dev * SPEC)
    return sums, jnp.transpose(powers, (2, 1, 0)), cross


def local(voltages, fir_taps, positions, cal_amp, cal_phase, cal_index, owner_counts, tile_owner):
    devices = lax.axis_size("chan")
    myself = lax.axis_index("chan")
    in_dev = voltages.shape[1]
    st_dev = in_dev // 2
    stations = st_dev * devices
    chan_dev = CH // devices
    per_group = AVG // chan_dev

    solutions = jnp.stack([cal_amp * jnp.cos(cal_phase), cal_amp * jnp.sin(cal_phase)])
    my_index = lax.dynamic_slice_in_dim(cal_index, myself * in_dev, in_dev, 0)
    my_index = my_index.reshape(st_dev, 2).T
    if chan_dev == AVG and st_dev % HALF == 0:
        outgoing, powers, crosses = channelise(
            voltages,
            fir_taps,
            my_index.reshape(1, in_dev),
            jnp.concatenate([solutions[0], solutions[1]], axis=1),
        )
    else:
        outgoing, powers, crosses = channelise_small(voltages, fir_taps, my_index, solutions, chan_dev)
    incoming = exchange(outgoing, 0)


    power_rows = jnp.transpose(powers, (2, 1, 0)).reshape(CH, in_dev) / jnp.float32(SPEC)
    offsets = jnp.cumsum(owner_counts) - owner_counts
    chan_ids = jnp.arange(CH, dtype=jnp.int32)
    member = (
        (chan_ids[None, :] >= offsets[:, None])
        & (chan_ids[None, :] < (offsets + owner_counts)[:, None])
    ).astype(jnp.float32)
    divisor = jnp.maximum(owner_counts, 1).astype(jnp.float32)
    sub_rows = jnp.dot(member, power_rows, precision=highest) / divisor[:, None]

    cross_power = 2.0 * jnp.sum(crosses.reshape(st_dev, GROUPS, AVG), axis=(0, 2))
    joined = jnp.transpose(incoming, (1, 0, 2, 3)).reshape(2, stations, chan_dev * SPEC)
    image = beam_images(joined, steering_axes(positions))

    tile_pix = PIX // devices
    device_ids = jnp.arange(devices, dtype=jnp.int32)
    tile_of = jnp.sum(
        jnp.where(tile_owner[None, :] == device_ids[:, None], device_ids[None, :], 0), axis=1
    )
    tiles = image.reshape(devices, tile_pix)[tile_of]
    last = jnp.concatenate(
        [tiles, sub_rows, jnp.broadcast_to(cross_power[None], (devices, GROUPS))], axis=1
    )
    width = last.shape[1]
    padded = jnp.pad(last, ((0, 0), (0, 8 * LANES - width))).reshape(devices, 8, LANES)
    arrived = exchange(padded, 1).reshape(devices, 8 * LANES)[:, :width]
    scale = jnp.float32(1.0 / (SPEC * AVG) * math.sqrt(SPEC * AVG) / (2 * stations))
    pieces = jnp.sum(arrived[:, :tile_pix].reshape(GROUPS, per_group, tile_pix), axis=1)
    constant = jnp.sum(arrived[:, tile_pix + in_dev :], axis=0)
    result = scale * (pieces + constant[:, None])
    autos = arrived[:, tile_pix : tile_pix + in_dev].reshape(1, devices * in_dev)
    return (result[None], autos)


def solution(mesh):
    in_specs = (
        P(None, ("grp", "chan"), None),
        P(),
        P(),
        P("grp", None),
        P("grp", None),
        P(),
        P("grp"),
        P("grp"),
    )
    out_specs = (P(("grp", "chan"), None, None), P(("grp", "chan"), None))
    return jax.shard_map(local, mesh=mesh, in_specs=in_specs, out_specs=out_specs, check_vma=False)
```

```python
import math

import jax
import numpy as np
import jax.numpy as jnp
from jax import lax
from jax.experimental import pallas as pl
from jax.experimental.pallas import tpu as pltpu
from jax.sharding import PartitionSpec as P

CH = 256
AVG = 16
GROUPS = 16
SPEC = 32
TAPS = 16
SIDE = 64
PIX = 4096
NCAL = 256

highest = lax.Precision.HIGHEST


def dft_table(length):
    indices = np.arange(length, dtype=np.int64)
    angles = (indices[:, None] * indices[None, :] % length) * (2.0 * math.pi / length)
    cosine = np.cos(angles) / math.sqrt(length)
    sine_part = np.sin(angles) / math.sqrt(length)
    upper_half = np.stack([cosine, sine_part], axis=1)
    lower_half = np.stack([-sine_part, cosine], axis=1)
    return np.stack([upper_half, lower_half], axis=1).astype(jnp.bfloat16)


def polyphase(voltage, fir_taps):
    length = fir_taps.shape[1]
    window = voltage.reshape(voltage.shape[0], voltage.shape[1], -1, length)
    summed = jnp.zeros((voltage.shape[0], voltage.shape[1], SPEC, length), jnp.float32)
    for tap_index in range(TAPS):
        summed = summed + window[:, :, tap_index : tap_index + SPEC, :].astype(
            jnp.float32
        ) * fir_taps[tap_index].astype(jnp.float32)
    return summed.astype(jnp.bfloat16)


LANES = 128
STEP = 8
HALF = 16


def channelise_kernel(
    volt_ref, fir_ref, table_ref, index_ref, solution_ref, out_ref, power_ref, cross_ref,
    filt, spec, taps_ref, gain_ref, stage, sent, landed, own,
):
    count = stage.shape[1]
    blocks = SPEC // STEP
    me = lax.axis_index("chan")
    barrier = pltpu.get_barrier_semaphore()

    @pl.loop(1, count)
    def _(step):
        pl.semaphore_signal(
            barrier,
            inc=1,
            device_id={"chan": lax.rem(me + step, count)},
            device_id_type=pl.DeviceIdType.MESH,
        )

    pl.semaphore_wait(barrier, count - 1)

    def transfer(block, step, slot):
        peer = lax.rem(me + step, count)
        return pltpu.make_async_remote_copy(
            src_ref=stage.at[block, peer],
            dst_ref=out_ref.at[block, slot],
            send_sem=sent.at[block, step],
            recv_sem=landed.at[block, step],
            device_id={"chan": peer},
            device_id_type=pl.DeviceIdType.MESH,
        )

    def keep_own(block):
        return pltpu.make_async_copy(stage.at[block, me], out_ref.at[block, me], own.at[block])

    length = fir_ref.shape[1]
    in_dev = volt_ref.shape[1]
    st_dev = in_dev // 2
    row_blocks = in_dev // HALF
    lane_blocks = length // LANES
    power_ref[...] = jnp.zeros_like(power_ref)
    cross_ref[...] = jnp.zeros_like(cross_ref)
    fir = fir_ref[...].astype(jnp.float32)
    for t in range(TAPS):
        taps_ref[t] = jnp.broadcast_to(fir[t : t + 1], (8, length))
    chosen = (
        lax.broadcasted_iota(jnp.int32, (NCAL, in_dev), 0) == index_ref[...]
    ).astype(jnp.float32)
    picked = lax.dot_general(
        chosen,
        solution_ref[...],
        (((0,), (0,)), ((), ())),
        precision=highest,
        preferred_element_type=jnp.float32,
    )
    column_ids = lax.broadcasted_iota(jnp.int32, (2 * GROUPS, length), 0)
    group_ids = lax.broadcasted_iota(jnp.int32, (2 * GROUPS, length), 1) // AVG
    for q in range(2):
        spread = (column_ids == group_ids + q * GROUPS).astype(jnp.float32)
        gains = jnp.dot(picked, spread, precision=highest, preferred_element_type=jnp.float32)
        gain_ref[q] = gains[:st_dev]
        gain_ref[2 + q] = gains[st_dev:]

    @pl.loop(0, SPEC // STEP)
    def _(block):
        first = block * STEP

        @pl.loop(0, 2 * row_blocks * lane_blocks)
        def _(turn):
            part = turn // (row_blocks * lane_blocks)
            row = pl.multiple_of(turn // lane_blocks % row_blocks * HALF, HALF)
            lane = pl.multiple_of(turn % lane_blocks * LANES, LANES)
            sums = [[None, None] for _ in range(STEP)]
            taps = [taps_ref[t, :, pl.ds(lane, LANES)] for t in range(TAPS)]
            for window in range(STEP + TAPS - 1):
                start = pl.multiple_of((first + window) * length + lane, LANES)
                both = volt_ref[part, pl.ds(row, HALF), pl.ds(start, LANES)].astype(jnp.float32)
                for half in range(2):
                    value = both[half * 8 : half * 8 + 8]
                    for s in range(max(0, window - TAPS + 1), min(STEP, window + 1)):
                        term = value * taps[window - s]
                        sums[s][half] = term if sums[s][half] is None else sums[s][half] + term
            column = pl.multiple_of(part * length + lane, LANES)
            for s in range(STEP):
                filt[s, pl.ds(row, HALF), pl.ds(column, LANES)] = jnp.concatenate(
                    sums[s], axis=0
                ).astype(jnp.bfloat16)

        rows = filt[...].reshape(STEP * in_dev, 2 * length)
        for column in range(2 * lane_blocks):
            product = jnp.dot(
                rows,
                table_ref[:, column * LANES : (column + 1) * LANES],
                preferred_element_type=jnp.float32,
            )
            spec[column] = product.astype(jnp.bfloat16).astype(jnp.float32)

        chunk = lax.broadcasted_iota(jnp.int32, (HALF, LANES), 1) // AVG
        for j in range(lane_blocks):
            lanes = slice(j * LANES, (j + 1) * LANES)
            for h in range(st_dev // HALF):
                st_rows = slice(h * HALF, (h + 1) * HALF)
                gre0, gim0, gre1, gim1 = (gain_ref[n, st_rows, lanes] for n in range(4))
                reals, imags = [], []
                power0 = power_ref[0, st_rows, lanes]
                power1 = power_ref[1, st_rows, lanes]
                cross = cross_ref[st_rows, lanes]
                for s in range(STEP):
                    base = s * in_dev + h * 2 * HALF
                    re0 = spec[j, pl.ds(base, HALF, stride=2), :]
                    re1 = spec[j, pl.ds(base + 1, HALF, stride=2), :]
                    im0 = spec[lane_blocks + j, pl.ds(base, HALF, stride=2), :]
                    im1 = spec[lane_blocks + j, pl.ds(base + 1, HALF, stride=2), :]
                    power0 = power0 + (re0 * re0 + im0 * im0)
                    power1 = power1 + (re1 * re1 + im1 * im1)
                    cre0 = re0 * gre0 - im0 * gim0
                    cim0 = re0 * gim0 + im0 * gre0
                    cre1 = re1 * gre1 - im1 * gim1
                    cim1 = re1 * gim1 + im1 * gre1
                    cross = cross + (cre0 * cre1 + cim0 * cim1)
                    reals.append(cre0 + cre1)
                    imags.append(cim0 + cim1)
                power_ref[0, st_rows, lanes] = power0
                power_ref[1, st_rows, lanes] = power1
                cross_ref[st_rows, lanes] = cross
                for q, planes in enumerate((reals, imags)):
                    bit = 1
                    while bit < STEP:
                        keep = (chunk // bit) % 2 == 0
                        for s in range(STEP):
                            if s & bit:
                                continue
                            low, high = planes[s], planes[s + bit]
                            shift = bit * AVG
                            planes[s] = jnp.where(keep, low, pltpu.roll(high, shift, 1))
                            planes[s + bit] = jnp.where(keep, pltpu.roll(low, LANES - shift, 1), high)
                        bit *= 2
                    for d in range(STEP):
                        stage[block, j * STEP + d, q, st_rows, :] = planes[d].astype(jnp.bfloat16)

        keep_own(block).start()

        @pl.loop(1, count)
        def _(step):
            transfer(block, step, me).start()

    @pl.loop(0, blocks)
    def _(block):
        keep_own(block).wait()

        @pl.loop(1, count)
        def _(step):
            transfer(block, step, lax.rem(me + count - step, count)).wait()


def image_kernel(data_ref, steer_ref, out_ref, even_ref, odd_ref, along, turned):
    stations, depth = data_ref.shape[1], data_ref.shape[2]
    along[:, :depth] = data_ref[0]
    along[:, depth:] = data_ref[1]
    turned[:, :depth] = data_ref[1]
    turned[:, depth:] = -data_ref[0]
    contract = (((1,), (1,)), ((), ()))
    tall = 256

    @pl.loop(0, stations // tall)
    def _(block):
        rows = pl.ds(pl.multiple_of(block * tall, tall), tall)
        even = lax.dot_general(along[rows, :], along[...], contract, preferred_element_type=jnp.float32)
        odd = lax.dot_general(turned[rows, :], along[...], contract, preferred_element_type=jnp.float32)
        row_ids = lax.broadcasted_iota(jnp.int32, (tall, stations), 0) + block * tall
        same = row_ids == lax.broadcasted_iota(jnp.int32, (tall, stations), 1)
        even_ref[rows, :] = jnp.where(same, 0.0, even).astype(jnp.bfloat16)
        odd_ref[rows, :] = jnp.where(same, 0.0, -2.0 * odd).astype(jnp.bfloat16)

    tile = out_ref.shape[1]
    lines = tile // SIDE

    @pl.loop(0, out_ref.shape[0], unroll=4)
    def _(block):
        cosines, sines = [], []
        for line in range(lines):
            u = block * lines + line
            east_cos = steer_ref[0, pl.ds(u, 1), :]
            east_sin = steer_ref[1, pl.ds(u, 1), :]
            cosines.append(east_cos * steer_ref[2] - east_sin * steer_ref[3])
            sines.append(east_sin * steer_ref[2] + east_cos * steer_ref[3])
        cosine = jnp.concatenate(cosines, axis=0)
        sine = jnp.concatenate(sines, axis=0)
        cos16, sin16 = cosine.astype(jnp.bfloat16), sine.astype(jnp.bfloat16)
        first = jnp.dot(cos16, even_ref[...], preferred_element_type=jnp.float32)
        first = first + jnp.dot(sin16, odd_ref[...], preferred_element_type=jnp.float32)
        second = jnp.dot(sin16, even_ref[...], preferred_element_type=jnp.float32)
        terms = cosine * first + sine * second
        folded = terms[:, :LANES]
        for j in range(1, stations // LANES):
            folded = folded + terms[:, j * LANES : (j + 1) * LANES]
        out_ref[pl.ds(block, 1), :] = jnp.sum(folded.T, axis=0, keepdims=True)


def exchange_kernel(source_ref, target_ref, sent, landed, own):
    count = source_ref.shape[0]
    me = lax.axis_index("chan")
    barrier = pltpu.get_barrier_semaphore()

    @pl.loop(1, count)
    def _(step):
        pl.semaphore_signal(
            barrier,
            inc=1,
            device_id={"chan": lax.rem(me + step, count)},
            device_id_type=pl.DeviceIdType.MESH,
        )

    local_copy = pltpu.make_async_copy(source_ref.at[me], target_ref.at[me], own)
    local_copy.start()
    pl.semaphore_wait(barrier, count - 1)

    def transfer(step, slot):
        peer = lax.rem(me + step, count)
        return pltpu.make_async_remote_copy(
            src_ref=source_ref.at[peer],
            dst_ref=target_ref.at[slot],
            send_sem=sent.at[step],
            recv_sem=landed.at[step],
            device_id={"chan": peer},
            device_id_type=pl.DeviceIdType.MESH,
        )

    @pl.loop(1, count)
    def _(step):
        transfer(step, me).start()

    local_copy.wait()

    @pl.loop(1, count)
    def _(step):
        transfer(step, lax.rem(me + count - step, count)).wait()


def exchange(blocks, number):
    count = blocks.shape[0]
    if count > 16:
        return lax.all_to_all(blocks, "chan", split_axis=0, concat_axis=0, tiled=True)
    vmem = pl.BlockSpec(memory_space=pltpu.VMEM)
    return pl.pallas_call(
        exchange_kernel,
        out_shape=jax.ShapeDtypeStruct(blocks.shape, blocks.dtype),
        in_specs=[vmem],
        out_specs=vmem,
        scratch_shapes=[
            pltpu.SemaphoreType.DMA((count,)),
            pltpu.SemaphoreType.DMA((count,)),
            pltpu.SemaphoreType.DMA,
        ],
        compiler_params=pltpu.CompilerParams(
            collective_id=number, has_side_effects=True, vmem_limit_bytes=16 * 1024 * 1024
        ),
        name="exchange",
    )(blocks)


def steering_axes(positions):
    steps = (jnp.arange(SIDE, dtype=jnp.float32) - SIDE // 2) / jnp.float32(SIDE)
    phases = jnp.float32(2.0 * math.pi) * (positions[:, None, :] * steps[None, :, None])
    stations = positions.shape[1]
    return jnp.stack([jnp.cos(phases), jnp.sin(phases)], axis=1).reshape(4, SIDE, stations)


def beam_images(joined, steer):
    stations, depth = joined.shape[1], joined.shape[2]
    vmem = pl.BlockSpec(memory_space=pltpu.VMEM)
    return pl.pallas_call(
        image_kernel,
        out_shape=jax.ShapeDtypeStruct((PIX // 256, 256), jnp.float32),
        in_specs=[vmem, vmem],
        out_specs=vmem,
        scratch_shapes=[
            pltpu.VMEM((stations, stations), jnp.bfloat16),
            pltpu.VMEM((stations, stations), jnp.bfloat16),
            pltpu.VMEM((stations, 2 * depth), jnp.bfloat16),
            pltpu.VMEM((stations, 2 * depth), jnp.bfloat16),
        ],
        compiler_params=pltpu.CompilerParams(vmem_limit_bytes=36 * 1024 * 1024),
        name="beam_images",
    )(joined, steer)


def channelise(voltages, fir_taps, my_index, solutions):
    in_dev = voltages.shape[1]
    st_dev = in_dev // 2
    table = jnp.asarray(np.transpose(dft_table(CH), (2, 3, 1, 0)).reshape(2 * CH, 2 * CH))
    vmem = pl.BlockSpec(memory_space=pltpu.VMEM)
    return pl.pallas_call(
        channelise_kernel,
        out_shape=[
            jax.ShapeDtypeStruct((SPEC // STEP, GROUPS, 2, st_dev, LANES), jnp.bfloat16),
            jax.ShapeDtypeStruct((2, st_dev, CH), jnp.float32),
            jax.ShapeDtypeStruct((st_dev, CH), jnp.float32),
        ],
        in_specs=[vmem] * 5,
        out_specs=[vmem] * 3,
        scratch_shapes=[
            pltpu.VMEM((STEP, in_dev, 2 * CH), jnp.bfloat16),
            pltpu.VMEM((2 * CH // LANES, STEP * in_dev, LANES), jnp.float32),
            pltpu.VMEM((TAPS, 8, CH), jnp.float32),
            pltpu.VMEM((4, st_dev, CH), jnp.float32),
            pltpu.VMEM((SPEC // STEP, GROUPS, 2, st_dev, LANES), jnp.bfloat16),
            pltpu.SemaphoreType.DMA((SPEC // STEP, GROUPS)),
            pltpu.SemaphoreType.DMA((SPEC // STEP, GROUPS)),
            pltpu.SemaphoreType.DMA((SPEC // STEP,)),
        ],
        compiler_params=pltpu.CompilerParams(
            collective_id=0, has_side_effects=True, vmem_limit_bytes=32 * 1024 * 1024
        ),
        name="channelise",
    )(voltages, fir_taps, table, my_index, solutions)


def channelise_small(voltages, fir_taps, my_index, solutions, chan_dev):
    in_dev = voltages.shape[1]
    st_dev = in_dev // 2
    spectra = jnp.einsum(
        "qrk,cpqk->cpr",
        polyphase(voltages, fir_taps).reshape(2, in_dev * SPEC, CH),
        dft_table(CH),
        preferred_element_type=jnp.float32,
    ).astype(jnp.bfloat16)
    values = spectra.astype(jnp.float32).reshape(GROUPS, AVG, 2, st_dev, 2, SPEC)
    powers = jnp.sum(values * values, axis=(2, 5)).reshape(CH, st_dev, 2)
    selection = (my_index.T[..., None] == jnp.arange(NCAL, dtype=jnp.int32)).astype(jnp.float32)
    gains = jnp.einsum("kpn,qng->qgkp", selection, solutions, precision=highest)
    gre, gim = gains[:, :, None, :, :, None]
    cal_re = values[:, :, 0] * gre - values[:, :, 1] * gim
    cal_im = values[:, :, 0] * gim + values[:, :, 1] * gre
    sums = jnp.stack(
        [cal_re[:, :, :, 0] + cal_re[:, :, :, 1], cal_im[:, :, :, 0] + cal_im[:, :, :, 1]]
    ).astype(jnp.bfloat16)
    crossed = cal_re[:, :, :, 0] * cal_re[:, :, :, 1] + cal_im[:, :, :, 0] * cal_im[:, :, :, 1]
    cross = jnp.sum(crossed, axis=3).reshape(CH, st_dev).T
    sums = jnp.transpose(
        sums.reshape(2, CH // chan_dev, chan_dev, st_dev, SPEC), (1, 0, 3, 2, 4)
    ).reshape(CH // chan_dev, 2, st_dev, chan_dev * SPEC)
    return sums, jnp.transpose(powers, (2, 1, 0)), cross


def local(voltages, fir_taps, positions, cal_amp, cal_phase, cal_index, owner_counts, tile_owner):
    devices = lax.axis_size("chan")
    myself = lax.axis_index("chan")
    in_dev = voltages.shape[1]
    st_dev = in_dev // 2
    stations = st_dev * devices
    chan_dev = CH // devices
    per_group = AVG // chan_dev

    solutions = jnp.stack([cal_amp * jnp.cos(cal_phase), cal_amp * jnp.sin(cal_phase)])
    my_index = lax.dynamic_slice_in_dim(cal_index, myself * in_dev, in_dev, 0)
    my_index = my_index.reshape(st_dev, 2).T
    if chan_dev == AVG and st_dev % HALF == 0:
        incoming, powers, crosses = channelise(
            voltages,
            fir_taps,
            my_index.reshape(1, in_dev),
            jnp.concatenate([solutions[0], solutions[1]], axis=1),
        )
    else:
        outgoing, powers, crosses = channelise_small(voltages, fir_taps, my_index, solutions, chan_dev)
        incoming = exchange(outgoing, 0)[None]


    power_rows = jnp.transpose(powers, (2, 1, 0)).reshape(CH, in_dev) / jnp.float32(SPEC)
    offsets = jnp.cumsum(owner_counts) - owner_counts
    chan_ids = jnp.arange(CH, dtype=jnp.int32)
    member = (
        (chan_ids[None, :] >= offsets[:, None])
        & (chan_ids[None, :] < (offsets + owner_counts)[:, None])
    ).astype(jnp.float32)
    divisor = jnp.maximum(owner_counts, 1).astype(jnp.float32)
    sub_rows = jnp.dot(member, power_rows, precision=highest) / divisor[:, None]

    cross_power = 2.0 * jnp.sum(crosses.reshape(st_dev, GROUPS, AVG), axis=(0, 2))
    joined = jnp.transpose(incoming, (2, 1, 3, 0, 4)).reshape(2, stations, chan_dev * SPEC)
    image = beam_images(joined, steering_axes(positions))

    tile_pix = PIX // devices
    device_ids = jnp.arange(devices, dtype=jnp.int32)
    tile_of = jnp.sum(
        jnp.where(tile_owner[None, :] == device_ids[:, None], device_ids[None, :], 0), axis=1
    )
    tiles = image.reshape(devices, tile_pix)[tile_of]
    last = jnp.concatenate(
        [tiles, sub_rows, jnp.broadcast_to(cross_power[None], (devices, GROUPS))], axis=1
    )
    width = last.shape[1]
    padded = jnp.pad(last, ((0, 0), (0, 8 * LANES - width))).reshape(devices, 8, LANES)
    arrived = exchange(padded, 1).reshape(devices, 8 * LANES)[:, :width]
    scale = jnp.float32(1.0 / (SPEC * AVG) * math.sqrt(SPEC * AVG) / (2 * stations))
    pieces = jnp.sum(arrived[:, :tile_pix].reshape(GROUPS, per_group, tile_pix), axis=1)
    constant = jnp.sum(arrived[:, tile_pix + in_dev :], axis=0)
    result = scale * (pieces + constant[:, None])
    autos = arrived[:, tile_pix : tile_pix + in_dev].reshape(1, devices * in_dev)
    return (result[None], autos)


def solution(mesh):
    in_specs = (
        P(None, ("grp", "chan"), None),
        P(),
        P(),
        P("grp", None),
        P("grp", None),
        P(),
        P("grp"),
        P("grp"),
    )
    out_specs = (P(("grp", "chan"), None, None), P(("grp", "chan"), None))
    return jax.shard_map(local, mesh=mesh, in_specs=in_specs, out_specs=out_specs, check_vma=False)
```
